32 devices in a mesh: grp: 2 (over y), ex: 8 (over z, x), dim: 2 (over core).
Axes of the slice: x: 2, y: 2, z: 4, core: 2. Of those that a mesh axis runs over, the one named last changes fastest.
Arguments:
- queries: bfloat16 [48, 16384], P('ex', 'dim'), may hold values from -6 to 6
- train_grads: bfloat16 [2048, 16384], P(('grp', 'ex'), 'dim'), parts along dimension 0, may hold values from -0.046875 to 0.046875
- precond: bfloat16 [16384, 64], P('dim'), may hold values from -0.03 to 3, as said below
Outputs:
- scores: float32 [2048, 48], P(('grp', 'ex'), 'dim'), parts along dimension 0
The draws below stay inside these ranges and needn't reach their ends.
There are 2 independent parts, one for each index of `grp`. The reference program is written for one: setup_inputs(seed, part) draws one part's arguments, and reference() takes and returns one part's arrays. A program takes and returns all parts, laid end to end along the dimension named above; an argument that names none is the same for every part. Nothing has to cross between parts.
Inputs may be any that keep to these rules, and one draw needn't show every extreme that they name: `precond`: entries of the preconditioner blocks.
All inputs are finite; a program needn't handle non-finite values.
Results may differ from the reference program's by a relative error of at most 0.0029.
Values may be sent and summed in bfloat16 or wider, within the bound.
No kernel may reach another device: no remote copies, remote signals or barrier semaphores. Data moves between devices by JAX's collectives and lax.ppermute only.
A program may use at most 64 MiB of HBM per device.

```python
import jax
import jax.numpy as jnp

K = 16384
PB = 64
TRAIN = 1024
NQ = 48


def draw_precond(key, part):
    key = jax.random.fold_in(key, 7)
    scale_key, coupling_key = jax.random.split(key)
    block_count = K // PB
    logs = jax.random.uniform(scale_key, (K,), jnp.float32, jnp.log(0.3), jnp.log(3.0))
    scales = jnp.exp(logs)
    coupling = jax.random.uniform(coupling_key, (block_count, PB, PB), jnp.float32, -1.0, 1.0)
    symmetric = (coupling + jnp.swapaxes(coupling, 1, 2)) * (0.5 / 140.0)
    identity = jnp.eye(PB, dtype=jnp.float32)
    unit_form = identity + symmetric * (1.0 - identity)
    roots = jnp.sqrt(scales).reshape(block_count, PB)
    matrices = roots[:, :, None] * unit_form * roots[:, None, :]
    return matrices.reshape(K, PB).astype(jnp.bfloat16)


def level_of(key, extent, pieces, low, largest):
    loudness, own = 1.0, jax.random.fold_in(key, 6)
    for dim, shards_of in pieces:
        steps = jnp.exp(jax.random.uniform(jax.random.fold_in(own, dim), (shards_of,), jnp.float32, low / len(pieces), largest / len(pieces)))
        loudness = loudness * jnp.repeat(steps, extent[dim] // shards_of).reshape([-1 if axis == dim else 1 for axis in range(len(extent))])
    return loudness


def scatter_about(stream_key, dims, spread, reach, cuts=(), kind=jnp.bfloat16):
    entries = spread * jax.random.normal(stream_key, dims, jnp.float32)
    if cuts:
        entries = entries * level_of(stream_key, dims, cuts, -0.22, 0.18)
    return jnp.clip(entries, -reach, reach).astype(kind)


def setup_inputs(seed: int = 0, part: int = 0) -> dict:
    key_list = jax.random.split(jax.random.key(seed), 4)
    own_keys = jax.random.split(jax.random.fold_in(key_list[3], part), 4)
    queries = scatter_about(key_list[0], (NQ, K), 1.0, 6.0, ((0, 8), (1, 2)))
    train_grads = scatter_about(own_keys[1], (TRAIN, K), K ** -0.5, 0.046875, ((0, 8), (1, 2)))
    precond = draw_precond(jax.random.fold_in(key_list[3], 71), part)
    return {"queries": queries, "train_grads": train_grads, "precond": precond}


def reference(queries, train_grads, precond):
    block_count = K // PB
    query_blocks = queries.astype(jnp.float32).reshape(NQ, block_count, PB)
    matrices = precond.astype(jnp.float32).reshape(block_count, PB, PB)
    conditioned = jnp.einsum("qbi,bij->qbj", query_blocks, matrices)
    conditioned = conditioned.reshape(NQ, K).astype(jnp.bfloat16)
    return jnp.dot(train_grads, conditioned.T, preferred_element_type=jnp.float32)
```

```python
import math

import jax
import jax.numpy as jnp
from jax import lax
from jax.experimental import pallas as pl
from jax.experimental.pallas import tpu as pltpu
from jax.sharding import PartitionSpec as P

LANES = 256
FOLD = 8
CONTRACT_LAST = (((1,), (1,)), ((), ()))
VMEM_LIMIT = 40 * 1024 * 1024


def ring_scores(queries, train_grads, precond):
    cycle_size = lax.axis_size("ex")
    dim_size = lax.axis_size("dim")
    query_rows, dims_dev = queries.shape
    train_rows = train_grads.shape[0]
    block_size = precond.shape[1]
    all_queries = query_rows * cycle_size
    matrices = precond.reshape(dims_dev // block_size, block_size, block_size)
    grouped = queries.reshape(query_rows, dims_dev // block_size, block_size)
    own_rows = jnp.einsum("qbi,bij->qbj", grouped, matrices, preferred_element_type=jnp.float32)
    own_rows = own_rows.reshape(query_rows, dims_dev).astype(jnp.bfloat16)
    group_len = math.gcd(cycle_size, 8)
    my_index = lax.axis_index("ex")
    route = [(i, (i + 1) % cycle_size) for i in range(cycle_size)]

    def score_group(running, held, first_step):
        score_tile = lax.dot_general(
            train_grads, jnp.concatenate(held, 0), CONTRACT_LAST, preferred_element_type=jnp.float32
        )
        for offset in range(group_len):
            source = (my_index - first_step - offset) % cycle_size
            running = lax.dynamic_update_slice(
                running,
                score_tile[:, offset * query_rows : (offset + 1) * query_rows],
                (jnp.int32(0), source * query_rows),
            )
        return running

    moving = own_rows
    held = [moving]
    for _ in range(1, group_len):
        moving = lax.ppermute(moving, "ex", route)
        held.append(moving)
    running = jnp.zeros((train_rows, all_queries), jnp.float32)
    running = score_group(running, held, jnp.int32(0))

    def cycle_step(group, carry):
        moving, running = carry
        held = []
        for _ in range(group_len):
            moving = lax.ppermute(moving, "ex", route)
            held.append(moving)
        return (moving, score_group(running, held, (group * group_len).astype(jnp.int32)))

    moving, partial_value = lax.fori_loop(1, cycle_size // group_len, cycle_step, (moving, running))
    summed = lax.psum(partial_value, "dim")
    half_cols = all_queries // dim_size
    return lax.dynamic_slice_in_dim(summed, lax.axis_index("dim") * half_cols, half_cols, 1)


def fold_kernel(train_ref, precond_ref, folded_ref):
    train_rows, dims = train_ref.shape
    block = precond_ref.shape[0]
    row_block = lax.broadcasted_iota(jnp.int32, (LANES, LANES), 0) // block
    col_block = lax.broadcasted_iota(jnp.int32, (LANES, LANES), 1) // block
    diagonal = row_block == col_block
    for chunk in range(dims // LANES):
        at = pl.ds(chunk * LANES, LANES)
        stacked = jnp.concatenate([precond_ref[:, at]] * (LANES // block), 0)
        matrix = jnp.where(diagonal, stacked, jnp.zeros_like(stacked))
        value = jnp.dot(train_ref[:, at], matrix, preferred_element_type=jnp.float32)
        head = value.astype(jnp.bfloat16)
        folded_ref[0:train_rows, at] = head
        rest = value - head.astype(jnp.float32)
        folded_ref[train_rows : 2 * train_rows, at] = rest.astype(jnp.bfloat16)


def partial_scores(folded_ref, blocks):
    joined = jnp.concatenate(blocks, 0)
    rows, width = joined.shape
    part = lax.broadcasted_iota(jnp.int32, (rows, width), 0) % FOLD
    total = None
    for k in range(FOLD):
        masked = jnp.where(part == k, joined, jnp.zeros_like(joined))
        term = lax.dot_general(
            masked,
            folded_ref[:, k * width : (k + 1) * width],
            CONTRACT_LAST,
            preferred_element_type=jnp.float32,
        )
        total = term if total is None else total + term
    train_rows = total.shape[1] // 2
    total = total[:, :train_rows] + total[:, train_rows:]
    return total.reshape(rows // FOLD, FOLD, train_rows).sum(1)


def in_order(pieces, flip):
    placed = []
    for slot in range(len(pieces)):
        chosen = pieces[slot]
        for other in range(1, len(pieces)):
            chosen = jnp.where(flip == other, pieces[slot ^ other], chosen)
        placed.append(chosen)
    return jnp.concatenate(placed, 0)


def near_kernel(folded_ref, own_ref, x_ref, z_ref, xz_ref, far_ref, near_ref, first_ref):
    scores = partial_scores(folded_ref, [r[...] for r in (own_ref, x_ref, z_ref, xz_ref, far_ref)])
    count = scores.shape[0] // 5
    pieces = [scores[i * count : (i + 1) * count] for i in range(5)]
    near_ref[...] = in_order(pieces[:4], lax.rem(lax.axis_index("ex"), 4))
    first_ref[...] = pieces[4]


def far_kernel(folded_ref, x_ref, y_ref, xy_ref, near_ref, first_ref, keep_ref, send_ref):
    scores = partial_scores(folded_ref, [r[...] for r in (x_ref, y_ref, xy_ref)])
    count = scores.shape[0] // 3
    pieces = [first_ref[...]] + [scores[i * count : (i + 1) * count] for i in range(3)]
    place = lax.axis_index("ex")
    flip = lax.rem(place, 4)
    flip = jnp.where(lax.axis_index("grp") == 1, flip ^ 2, flip)
    far = in_order(pieces, flip)
    near = near_ref[...]
    near_stays = lax.axis_index("dim") == place // 4
    keep_ref[...] = jnp.where(near_stays, near, far)
    send_ref[...] = jnp.where(near_stays, far, near)


def call(kernel, outs, args, flops):
    vmem = pl.BlockSpec(memory_space=pltpu.VMEM)
    moved = sum(a.size * a.dtype.itemsize for a in args)
    return pl.pallas_call(
        kernel,
        out_shape=outs,
        in_specs=[vmem] * len(args),
        out_specs=jax.tree.map(lambda _: vmem, outs),
        compiler_params=pltpu.CompilerParams(vmem_limit_bytes=VMEM_LIMIT),
        cost_estimate=pl.CostEstimate(flops=flops, bytes_accessed=moved, transcendentals=0),
    )(*args)


def crossing_scores(queries, train_grads, precond):
    query_rows, dims = queries.shape
    train_rows = train_grads.shape[0]

    def swap(value, mask):
        return lax.ppermute(value, "ex", [(i, i ^ mask) for i in range(8)])

    def swap_both(value, place):
        route = [(g * 8 + e, place(g, e)) for g in range(2) for e in range(8)]
        return lax.ppermute(value, ("grp", "ex"), route)

    own = queries.reshape(query_rows * FOLD, dims // FOLD)
    far = swap_both(own, lambda g, e: g * 8 + (e ^ (6 if g else 4)))
    near_x = swap(own, 1)
    near_z = swap(own, 2)
    near_xz = swap(near_x, 2)
    far_x = swap(far, 1)
    far_xy = swap_both(far, lambda g, e: (1 - g) * 8 + (e ^ 1))
    far_y = lax.ppermute(far, "grp", [(0, 1), (1, 0)])

    folded = call(
        fold_kernel,
        jax.ShapeDtypeStruct((2 * train_rows, dims), jnp.bfloat16),
        (train_grads, precond.T),
        2 * train_rows * dims * LANES,
    )
    quarter = jax.ShapeDtypeStruct((query_rows, train_rows), jnp.float32)
    half = jax.ShapeDtypeStruct((query_rows * 4, train_rows), jnp.float32)
    flops = 4 * train_rows * dims * query_rows * FOLD
    near, first = call(
        near_kernel, (half, quarter), (folded, own, near_x, near_z, near_xz, far), 5 * flops
    )
    keep, send = call(
        far_kernel, (half, half), (folded, far_x, far_y, far_xy, near, first), 3 * flops
    )
    return (keep + lax.ppermute(send, "dim", [(0, 1), (1, 0)])).T


def solution(mesh):
    placed = (P("ex", "dim"), P(("grp", "ex"), "dim"), P("dim", None))
    crossing = mesh.shape["grp"] == 2 and mesh.shape["ex"] == 8 and mesh.shape["dim"] == 2
    return jax.shard_map(
        crossing_scores if crossing else ring_scores,
        mesh=mesh,
        in_specs=placed,
        out_specs=P(("grp", "ex"), "dim"),
        check_vma=False,
    )
```

```python
import math

import jax
import jax.numpy as jnp
from jax import lax
from jax.experimental import pallas as pl
from jax.experimental.pallas import tpu as pltpu
from jax.sharding import PartitionSpec as P

LANES = 256
PACKED = 8
CONTRACT_LAST = (((1,), (1,)), ((), ()))
VMEM_LIMIT = 40 * 1024 * 1024


def ring_scores(queries, train_grads, precond):
    cycle_size = lax.axis_size("ex")
    dim_size = lax.axis_size("dim")
    query_rows, dims_dev = queries.shape
    train_rows = train_grads.shape[0]
    block_size = precond.shape[1]
    all_queries = query_rows * cycle_size
    matrices = precond.reshape(dims_dev // block_size, block_size, block_size)
    grouped = queries.reshape(query_rows, dims_dev // block_size, block_size)
    own_rows = jnp.einsum("qbi,bij->qbj", grouped, matrices, preferred_element_type=jnp.float32)
    own_rows = own_rows.reshape(query_rows, dims_dev).astype(jnp.bfloat16)
    group_len = math.gcd(cycle_size, 8)
    my_index = lax.axis_index("ex")
    route = [(i, (i + 1) % cycle_size) for i in range(cycle_size)]

    def score_group(running, held, first_step):
        score_tile = lax.dot_general(
            train_grads, jnp.concatenate(held, 0), CONTRACT_LAST, preferred_element_type=jnp.float32
        )
        for offset in range(group_len):
            source = (my_index - first_step - offset) % cycle_size
            running = lax.dynamic_update_slice(
                running,
                score_tile[:, offset * query_rows : (offset + 1) * query_rows],
                (jnp.int32(0), source * query_rows),
            )
        return running

    moving = own_rows
    held = [moving]
    for _ in range(1, group_len):
        moving = lax.ppermute(moving, "ex", route)
        held.append(moving)
    running = jnp.zeros((train_rows, all_queries), jnp.float32)
    running = score_group(running, held, jnp.int32(0))

    def cycle_step(group, carry):
        moving, running = carry
        held = []
        for _ in range(group_len):
            moving = lax.ppermute(moving, "ex", route)
            held.append(moving)
        return (moving, score_group(running, held, (group * group_len).astype(jnp.int32)))

    moving, partial_value = lax.fori_loop(1, cycle_size // group_len, cycle_step, (moving, running))
    summed = lax.psum(partial_value, "dim")
    half_cols = all_queries // dim_size
    return lax.dynamic_slice_in_dim(summed, lax.axis_index("dim") * half_cols, half_cols, 1)


def fold_kernel(train_ref, precond_ref, folded_ref):
    train_rows, dims = train_ref.shape
    block = precond_ref.shape[0]
    row_block = lax.broadcasted_iota(jnp.int32, (LANES, LANES), 0) // block
    col_block = lax.broadcasted_iota(jnp.int32, (LANES, LANES), 1) // block
    diagonal = row_block == col_block
    for chunk in range(dims // LANES):
        at = pl.ds(chunk * LANES, LANES)
        stacked = jnp.concatenate([precond_ref[:, at]] * (LANES // block), 0)
        matrix = jnp.where(diagonal, stacked, jnp.zeros_like(stacked))
        value = jnp.dot(train_ref[:, at], matrix, preferred_element_type=jnp.float32)
        head = value.astype(jnp.bfloat16)
        folded_ref[0:train_rows, at] = head
        rest = value - head.astype(jnp.float32)
        folded_ref[train_rows : 2 * train_rows, at] = rest.astype(jnp.bfloat16)


def pack_kernel(queries_ref, packed_ref):
    rows, dims = queries_ref.shape
    width = packed_ref.shape[1]
    each = width // (dims - width)
    main = queries_ref[:, :width].astype(jnp.float32)
    tail = queries_ref[:, width:].astype(jnp.float32)
    below = jnp.concatenate(
        [jnp.concatenate([tail[i : i + 1] for i in range(m, rows, each)], 0) for m in range(each)],
        1,
    )
    packed_ref[...] = jnp.concatenate([main, below], 0).astype(jnp.bfloat16)


def partial_scores(folded_ref, refs):
    width = refs[0].shape[1]
    dims = folded_ref.shape[1]
    tail = dims - width
    each = width // tail
    rows = width * PACKED // dims
    joined = jnp.concatenate([r[...].astype(jnp.float32) for r in refs], 0)
    tails = jnp.concatenate([joined[:, m * tail : (m + 1) * tail] for m in range(each)], 0)
    main = lax.dot_general(
        joined.astype(jnp.bfloat16),
        folded_ref[:, :width],
        CONTRACT_LAST,
        preferred_element_type=jnp.float32,
    )
    rest = lax.dot_general(
        tails.astype(jnp.bfloat16),
        folded_ref[:, width:],
        CONTRACT_LAST,
        preferred_element_type=jnp.float32,
    )
    train_rows = main.shape[1] // 2
    main = main[:, :train_rows] + main[:, train_rows:]
    rest = rest[:, :train_rows] + rest[:, train_rows:]
    scores = []
    for i in range(len(refs)):
        below = []
        for row in range(rows):
            at = (row % each * len(refs) + i) * PACKED + rows + row // each
            below.append(rest[at : at + 1])
        scores.append(main[i * PACKED : i * PACKED + rows] + jnp.concatenate(below, 0))
    return scores


def in_order(pieces, flip):
    placed = []
    for slot in range(len(pieces)):
        chosen = pieces[slot]
        for other in range(1, len(pieces)):
            chosen = jnp.where(flip == other, pieces[slot ^ other], chosen)
        placed.append(chosen)
    return jnp.concatenate(placed, 0)


def near_kernel(folded_ref, own_ref, xz_ref, z_ref, x_ref, far_ref, near_ref, first_ref):
    pieces = partial_scores(folded_ref, (own_ref, x_ref, z_ref, xz_ref, far_ref))
    near_ref[...] = in_order(pieces[:4], lax.rem(lax.axis_index("ex"), 4))
    first_ref[...] = pieces[4]


def far_kernel(folded_ref, x_ref, z_ref, y_ref, near_ref, first_ref, keep_ref, send_ref):
    pieces = [first_ref[...]] + partial_scores(folded_ref, (x_ref, z_ref, y_ref))
    place = lax.axis_index("ex")
    flip = lax.rem(place, 4)
    flip = flip ^ jnp.where(lax.axis_index("grp") == 1, 2, 1)
    far = in_order(pieces, flip)
    near = near_ref[...]
    near_stays = lax.axis_index("dim") == place // 4
    keep_ref[...] = jnp.where(near_stays, near, far)
    send_ref[...] = jnp.where(near_stays, far, near)


def call(kernel, outs, args, flops):
    vmem = pl.BlockSpec(memory_space=pltpu.VMEM)
    moved = sum(a.size * a.dtype.itemsize for a in args)
    return pl.pallas_call(
        kernel,
        out_shape=outs,
        in_specs=[vmem] * len(args),
        out_specs=jax.tree.map(lambda _: vmem, outs),
        compiler_params=pltpu.CompilerParams(vmem_limit_bytes=VMEM_LIMIT),
        cost_estimate=pl.CostEstimate(flops=flops, bytes_accessed=moved, transcendentals=0),
    )(*args)


def crossing_scores(queries, train_grads, precond):
    query_rows, dims = queries.shape
    train_rows = train_grads.shape[0]

    def swap(value, mask):
        return lax.ppermute(value, "ex", [(i, i ^ mask) for i in range(8)])

    def swap_both(value, place):
        route = [(g * 8 + e, place(g, e)) for g in range(2) for e in range(8)]
        return lax.ppermute(value, ("grp", "ex"), route)

    own = call(
        pack_kernel,
        jax.ShapeDtypeStruct((PACKED, query_rows * dims // PACKED), jnp.bfloat16),
        (queries,),
        5_000_000_000,
    )
    far = swap_both(own, lambda g, e: g * 8 + (e ^ (6 if g else 5)))
    folded = call(
        fold_kernel,
        jax.ShapeDtypeStruct((2 * train_rows, dims), jnp.bfloat16),
        (train_grads, precond.T),
        2 * train_rows * dims * LANES,
    )
    far, folded = lax.optimization_barrier((far, folded))
    far_x = swap(far, 1)
    far_z = swap(far, 2)
    far_y = lax.ppermute(far, "grp", [(0, 1), (1, 0)])
    near_x = swap(own, 1)
    near_z = swap(own, 2)
    near_xz = swap(own, 3)
    quarter = jax.ShapeDtypeStruct((query_rows, train_rows), jnp.float32)
    half = jax.ShapeDtypeStruct((query_rows * 4, train_rows), jnp.float32)
    flops = 4 * train_rows * dims * LANES
    near, first = call(
        near_kernel, (half, quarter), (folded, own, near_xz, near_z, near_x, far), flops
    )
    keep, send = call(far_kernel, (half, half), (folded, far_x, far_z, far_y, near, first), flops)
    return (keep + lax.ppermute(send, "dim", [(0, 1), (1, 0)])).T


def solution(mesh):
    placed = (P("ex", "dim"), P(("grp", "ex"), "dim"), P("dim", None))
    crossing = mesh.shape["grp"] == 2 and mesh.shape["ex"] == 8 and mesh.shape["dim"] == 2
    return jax.shard_map(
        crossing_scores if crossing else ring_scores,
        mesh=mesh,
        in_specs=placed,
        out_specs=P(("grp", "ex"), "dim"),
        check_vma=False,
    )
```

```python
import math

import jax
import jax.numpy as jnp
from jax import lax
from jax.experimental import pallas as pl
from jax.experimental.pallas import tpu as pltpu
from jax.sharding import PartitionSpec as P

LANES = 256
PACKED = 8
REST = jnp.float8_e5m2
REST_SCALE = 8192.0
CONTRACT_LAST = (((1,), (1,)), ((), ()))
VMEM_LIMIT = 40 * 1024 * 1024


def ring_scores(queries, train_grads, precond):
    cycle_size = lax.axis_size("ex")
    dim_size = lax.axis_size("dim")
    query_rows, dims_dev = queries.shape
    train_rows = train_grads.shape[0]
    block_size = precond.shape[1]
    all_queries = query_rows * cycle_size
    matrices = precond.reshape(dims_dev // block_size, block_size, block_size)
    grouped = queries.reshape(query_rows, dims_dev // block_size, block_size)
    own_rows = jnp.einsum("qbi,bij->qbj", grouped, matrices, preferred_element_type=jnp.float32)
    own_rows = own_rows.reshape(query_rows, dims_dev).astype(jnp.bfloat16)
    group_len = math.gcd(cycle_size, 8)
    my_index = lax.axis_index("ex")
    route = [(i, (i + 1) % cycle_size) for i in range(cycle_size)]

    def score_group(running, held, first_step):
        score_tile = lax.dot_general(
            train_grads, jnp.concatenate(held, 0), CONTRACT_LAST, preferred_element_type=jnp.float32
        )
        for offset in range(group_len):
            source = (my_index - first_step - offset) % cycle_size
            running = lax.dynamic_update_slice(
                running,
                score_tile[:, offset * query_rows : (offset + 1) * query_rows],
                (jnp.int32(0), source * query_rows),
            )
        return running

    moving = own_rows
    held = [moving]
    for _ in range(1, group_len):
        moving = lax.ppermute(moving, "ex", route)
        held.append(moving)
    running = jnp.zeros((train_rows, all_queries), jnp.float32)
    running = score_group(running, held, jnp.int32(0))

    def cycle_step(group, carry):
        moving, running = carry
        held = []
        for _ in range(group_len):
            moving = lax.ppermute(moving, "ex", route)
            held.append(moving)
        return (moving, score_group(running, held, (group * group_len).astype(jnp.int32)))

    moving, partial_value = lax.fori_loop(1, cycle_size // group_len, cycle_step, (moving, running))
    summed = lax.psum(partial_value, "dim")
    half_cols = all_queries // dim_size
    return lax.dynamic_slice_in_dim(summed, lax.axis_index("dim") * half_cols, half_cols, 1)


def fold_kernel(train_ref, precond_ref, head_ref, rest_ref):
    dims = train_ref.shape[1]
    block = precond_ref.shape[0]
    row_block = lax.broadcasted_iota(jnp.int32, (LANES, LANES), 0) // block
    col_block = lax.broadcasted_iota(jnp.int32, (LANES, LANES), 1) // block
    diagonal = row_block == col_block
    for chunk in range(dims // LANES):
        at = pl.ds(chunk * LANES, LANES)
        stacked = jnp.concatenate([precond_ref[:, at]] * (LANES // block), 0)
        matrix = jnp.where(diagonal, stacked, jnp.zeros_like(stacked))
        value = jnp.dot(train_ref[:, at], matrix, preferred_element_type=jnp.float32)
        head = value.astype(jnp.bfloat16)
        head_ref[:, at] = head
        rest_ref[:, at] = ((value - head.astype(jnp.float32)) * REST_SCALE).astype(REST)


def pack_kernel(queries_ref, packed_ref):
    rows, dims = queries_ref.shape
    width = packed_ref.shape[1]
    each = width // (dims - width)
    main = queries_ref[:, :width].astype(jnp.float32)
    tail = queries_ref[:, width:].astype(jnp.float32)
    below = jnp.concatenate(
        [jnp.concatenate([tail[i : i + 1] for i in range(m, rows, each)], 0) for m in range(each)],
        1,
    )
    packed_ref[...] = jnp.concatenate([main, below], 0).astype(jnp.bfloat16)


def rows_by_train(rows, head_ref, rest_ref, at):
    head = lax.dot_general(
        rows.astype(jnp.bfloat16), head_ref[:, at], CONTRACT_LAST, preferred_element_type=jnp.float32
    )
    rest = lax.dot_general(
        rows.astype(REST), rest_ref[:, at], CONTRACT_LAST, preferred_element_type=jnp.float32
    )
    return head + rest * (1.0 / REST_SCALE)


def partial_scores(head_ref, rest_ref, refs):
    width = refs[0].shape[1]
    dims = head_ref.shape[1]
    tail = dims - width
    each = width // tail
    rows = width * PACKED // dims
    joined = jnp.concatenate([r[...].astype(jnp.float32) for r in refs], 0)
    tails = jnp.concatenate([joined[:, m * tail : (m + 1) * tail] for m in range(each)], 0)
    main = rows_by_train(joined, head_ref, rest_ref, pl.ds(0, width))
    tails = rows_by_train(tails, head_ref, rest_ref, pl.ds(width, tail))
    scores = []
    for i in range(len(refs)):
        below = []
        for row in range(rows):
            at = (row % each * len(refs) + i) * PACKED + rows + row // each
            below.append(tails[at : at + 1])
        scores.append(main[i * PACKED : i * PACKED + rows] + jnp.concatenate(below, 0))
    return scores


def in_order(pieces, flip):
    placed = []
    for slot in range(len(pieces)):
        chosen = pieces[slot]
        for other in range(1, len(pieces)):
            chosen = jnp.where(flip == other, pieces[slot ^ other], chosen)
        placed.append(chosen)
    return jnp.concatenate(placed, 0)


def near_kernel(head_ref, rest_ref, own_ref, xz_ref, x_ref, z_ref, far_ref, near_ref, first_ref):
    pieces = partial_scores(head_ref, rest_ref, (own_ref, x_ref, z_ref, xz_ref, far_ref))
    near_ref[...] = in_order(pieces[:4], lax.rem(lax.axis_index("ex"), 4))
    first_ref[...] = pieces[4]


def far_kernel(head_ref, rest_ref, x_ref, z_ref, y_ref, near_ref, first_ref, keep_ref, send_ref):
    pieces = [first_ref[...]] + partial_scores(head_ref, rest_ref, (x_ref, z_ref, y_ref))
    place = lax.axis_index("ex")
    flip = lax.rem(place, 4)
    flip = flip ^ jnp.where(lax.axis_index("grp") == 1, 2, 1)
    far = in_order(pieces, flip)
    near = near_ref[...]
    near_stays = lax.axis_index("dim") == place // 4
    keep_ref[...] = jnp.where(near_stays, near, far)
    send_ref[...] = jnp.where(near_stays, far, near)


def call(kernel, outs, args, flops):
    vmem = pl.BlockSpec(memory_space=pltpu.VMEM)
    moved = sum(a.size * a.dtype.itemsize for a in args)
    return pl.pallas_call(
        kernel,
        out_shape=outs,
        in_specs=[vmem] * len(args),
        out_specs=jax.tree.map(lambda _: vmem, outs),
        compiler_params=pltpu.CompilerParams(vmem_limit_bytes=VMEM_LIMIT),
        cost_estimate=pl.CostEstimate(flops=flops, bytes_accessed=moved, transcendentals=0),
    )(*args)


def crossing_scores(queries, train_grads, precond):
    query_rows, dims = queries.shape
    train_rows = train_grads.shape[0]

    def swap(value, mask):
        return lax.ppermute(value, "ex", [(i, i ^ mask) for i in range(8)])

    def swap_both(value, place):
        route = [(g * 8 + e, place(g, e)) for g in range(2) for e in range(8)]
        return lax.ppermute(value, ("grp", "ex"), route)

    own = call(
        pack_kernel,
        jax.ShapeDtypeStruct((PACKED, query_rows * dims // PACKED), jnp.bfloat16),
        (queries,),
        5_000_000_000,
    )
    far = swap_both(own, lambda g, e: g * 8 + (e ^ (6 if g else 5)))
    head, rest = call(
        fold_kernel,
        (
            jax.ShapeDtypeStruct((train_rows, dims), jnp.bfloat16),
            jax.ShapeDtypeStruct((train_rows, dims), REST),
        ),
        (train_grads, precond.T),
        2 * train_rows * dims * LANES,
    )
    far, head, rest = lax.optimization_barrier((far, head, rest))
    far_x = swap(far, 1)
    far_z = swap(far, 2)
    far_y = lax.ppermute(far, "grp", [(0, 1), (1, 0)])
    near_x = swap(own, 1)
    near_z = swap(own, 2)
    near_xz = swap(own, 3)
    quarter = jax.ShapeDtypeStruct((query_rows, train_rows), jnp.float32)
    half = jax.ShapeDtypeStruct((query_rows * 4, train_rows), jnp.float32)
    flops = 4 * train_rows * dims * LANES
    near, first = call(
        near_kernel, (half, quarter), (head, rest, own, near_xz, near_x, near_z, far), flops
    )
    keep, send = call(far_kernel, (half, half), (head, rest, far_x, far_z, far_y, near, first), flops)
    return (keep + lax.ppermute(send, "dim", [(0, 1), (1, 0)])).T


def solution(mesh):
    placed = (P("ex", "dim"), P(("grp", "ex"), "dim"), P("dim", None))
    crossing = mesh.shape["grp"] == 2 and mesh.shape["ex"] == 8 and mesh.shape["dim"] == 2
    return jax.shard_map(
        crossing_scores if crossing else ring_scores,
        mesh=mesh,
        in_specs=placed,
        out_specs=P(("grp", "ex"), "dim"),
        check_vma=False,
    )
```
